32 devices in a mesh: rep: 2 (over x), node: 2 (over core), local: 8 (over z, y).
Axes of the slice: x: 2, y: 2, z: 4, core: 2. Of those that a mesh axis runs over, the one named last changes fastest.
Arguments:
- tokens: bfloat16 [4096, 3584], P(('rep', 'node', 'local')), parts along dimension 0, may hold values from -6 to 6
- expert_ids: int32 [4096, 2], P(('rep', 'node', 'local')), parts along dimension 0, may hold values from 0 to 7, all different within a row; in each aligned block of 128 rows (0 to 127, 128 to 255, ...) at most 80 rows name the same one
- route_weights: float32 [4096, 2], P(('rep', 'node', 'local')), parts along dimension 0, may hold values from 0.2 to 1
- gate_weight: bfloat16 [8, 3584, 1024], P('local', None, 'node'), may hold values from -0.09375 to 0.09375
- up_weight: bfloat16 [8, 3584, 1024], P('local', None, 'node'), may hold values from -0.09375 to 0.09375
- down_weight: bfloat16 [8, 1024, 3584], P('local', 'node'), may hold values from -0.1875 to 0.1875
Outputs:
- moe_output: bfloat16 [4096, 3584], P(('rep', 'node', 'local')), parts along dimension 0
The draws below stay inside these ranges and needn't reach their ends.
There are 2 independent parts, one for each index of `rep`. The reference program is written for one: setup_inputs(seed, part) draws one part's arguments, and reference() takes and returns one part's arrays. A program takes and returns all parts, laid end to end along the dimension named above; an argument that names none is the same for every part. Nothing has to cross between parts.
Inputs may be any that keep to these rules, and one draw needn't show every extreme that they name: `expert_ids`: each row names 2 different experts; within the 128 rows of one device no expert is named by more than 80 rows, a bound that some block reaches.
All inputs are finite; a program needn't handle non-finite values.
Results may differ from the reference program's by a relative error of at most 0.0058.
Values may be sent and summed in bfloat16 or wider, within the bound.
A program may use at most 128 MiB of HBM per device.

```python
import math
import jax
import jax.numpy as jnp
import numpy as np
from jax import lax

D = 3584
FF = 1024
TOPK = 2
TOK_DEV = 128
EXPERTS = 8
CAP = 80
TOKENS = 2048
N_NODE = 2
N_LOCAL = 8


def shard_levels(stream_key, dims, cuts, smallest, high):
    loudness = 1.0
    for axis_at, parts in cuts:
        heights = jax.random.uniform(jax.random.fold_in(jax.random.fold_in(stream_key, 6), axis_at), (parts,), jnp.float32, smallest / len(cuts), high / len(cuts))
        loudness = loudness * jnp.repeat(jnp.exp(heights), dims[axis_at] // parts).reshape((-1,) + (1,) * (len(dims) - 1 - axis_at))
    return loudness


def deal_out(rng, own, number, rows, amount, top, bound, skew):
    sequence = jax.random.permutation(rng, amount)
    packed, ordinary = shares(amount, rows * top, bound, skew, True), shares(amount, rows * top, bound, skew, False)
    places = jnp.arange(amount)

    def named(tallies, offset_by):
        used = int((tallies > 0).sum())
        fixed = max(1, used // 4)
        moved = fixed + (places - fixed + offset_by * (used - fixed)) % max(1, amount - fixed)
        return jnp.zeros((amount,), jnp.int32).at[sequence[jnp.where(places < fixed, places, moved)]].set(jnp.asarray(tallies, jnp.int32))

    tallies = jnp.where(number % 4 == 0, named(packed, number // 4), named(ordinary, number - number // 4 - 1))
    mixed = jax.random.permutation(jax.random.fold_in(own, 3), amount)
    giver, receiver = mixed[0:amount // 2 * 2:2], mixed[1:amount // 2 * 2:2]
    margin = jnp.minimum(tallies[giver] - 1, bound - tallies[receiver]) // 2
    margin = jnp.where((giver == sequence[0]) | (receiver == sequence[0]) | (tallies[receiver] == 0), 0, jnp.maximum(margin, 0))
    moved = jax.random.randint(jax.random.fold_in(own, 4), (amount // 2,), 0, 1 << 20) % (margin + 1)
    tallies = tallies.at[giver].add(-moved).at[receiver].add(moved)
    items = jnp.searchsorted(jnp.cumsum(tallies), jnp.arange(rows * top), side="right").astype(jnp.int32)
    table = items.reshape(top, rows).T
    table = table[jax.random.permutation(jax.random.fold_in(own, 1), rows)]
    offset_by = jax.random.randint(jax.random.fold_in(own, 2), (rows, 1), 0, top)
    return jnp.take_along_axis(table, (jnp.arange(top)[None, :] + offset_by) % top, axis=1)


def shares(number_of, total, limit, skew, full):
    portions = [(1 << 20) // math.isqrt(grade ** skew) + 1 for grade in range(1, number_of + 1)]
    largest = limit if full else min(limit, max(-(-total // number_of), total * portions[0] // sum(portions)))
    least = 1 if total - largest >= number_of - 1 else 0
    given, spare = [largest] + [least] * (number_of - 1), total - largest - least * (number_of - 1)
    while spare > 0:
        candidates = [i for i in range(1, number_of) if given[i] < largest] or [i for i in range(1, number_of) if given[i] < limit]
        whole, remaining = sum([portions[i] for i in candidates]), spare
        for i in candidates:
            addition = min(limit - given[i], max(1, remaining * portions[i] // whole), spare)
            given[i] = given[i] + addition
            spare = spare - addition
    return np.array(given)


def bell_draw(key, extent, spread, most, pieces=(), kind=jnp.bfloat16):
    level = shard_levels(key, extent, pieces, -0.22, 0.18) if pieces else 1.0
    drawn = jax.random.normal(key, extent, jnp.float32) * spread * level
    return jnp.minimum(jnp.maximum(drawn, -most), most).astype(kind)


def setup_inputs(seed: int = 0, part: int = 0) -> dict:
    seeds = jax.random.split(jax.random.key(seed), 7)
    part_splits = jax.random.split(jax.random.fold_in(seeds[6], part), 7)
    tokens = bell_draw(part_splits[0], (TOKENS, D), 1.0, 6.0, ((0, 16),))
    expert_ids_keys = jax.random.split(jax.random.fold_in(part_splits[1], 1), TOKENS // TOK_DEV)
    expert_ids_turns = jax.random.permutation(jax.random.fold_in(part_splits[1], 3), TOKENS // TOK_DEV)
    expert_ids = jax.vmap(lambda own, number: deal_out(jax.random.fold_in(part_splits[1], 2), own, number, TOK_DEV, EXPERTS, TOPK, CAP, 2))(expert_ids_keys, expert_ids_turns).reshape((TOKENS, TOPK))
    route_weights = jnp.clip(0.2 + 0.8 * jax.random.uniform(part_splits[2], (TOKENS, TOPK), jnp.float32) ** shard_levels(part_splits[2], (TOKENS, TOPK), ((0, 16),), -0.2, 0.2), 0.2, 1.0)
    gate_weight = bell_draw(seeds[3], (EXPERTS, D, FF), D ** -0.5, 0.09375, ((0, 8), (2, 2)))
    up_weight = bell_draw(seeds[4], (EXPERTS, D, FF), D ** -0.5, 0.09375, ((0, 8), (2, 2)))
    down_weight = bell_draw(seeds[5], (EXPERTS, FF, D), FF ** -0.5, 0.1875, ((0, 8), (1, 2)))
    return {"tokens": tokens, "expert_ids": expert_ids, "route_weights": route_weights, "gate_weight": gate_weight, "up_weight": up_weight, "down_weight": down_weight}


def reference(tokens, expert_ids, route_weights, gate_weight, up_weight, down_weight):
    token_total = tokens.shape[0]
    queue_len = min(token_total, N_NODE * N_LOCAL * CAP)

    def one_expert(accumulated, expert_id):
        selected = expert_ids == expert_id
        weight_sum = jnp.sum(jnp.where(selected, route_weights, jnp.zeros_like(route_weights)), axis=1)
        chosen = jnp.any(selected, axis=1)
        row_index = jnp.nonzero(chosen, size=queue_len, fill_value=0)[0].astype(jnp.int32)
        is_valid = jnp.arange(queue_len) < jnp.sum(chosen.astype(jnp.int32))
        picked = tokens[row_index]
        gate_act = jnp.dot(picked, gate_weight[expert_id], preferred_element_type=jnp.float32)
        up_act = jnp.dot(picked, up_weight[expert_id], preferred_element_type=jnp.float32)
        hidden = (jax.nn.silu(gate_act) * up_act).astype(jnp.bfloat16)
        expert_out = jnp.dot(hidden, down_weight[expert_id], preferred_element_type=jnp.float32).astype(jnp.bfloat16)
        row_weight = jnp.where(is_valid, weight_sum[row_index], jnp.zeros_like(weight_sum[row_index]))
        accumulated = accumulated.at[row_index].add(row_weight[:, None] * expert_out.astype(accumulated.dtype))
        return accumulated, None

    start = jnp.zeros((token_total, tokens.shape[1]), jnp.float32)
    accumulated, _ = lax.scan(one_expert, start, jnp.arange(EXPERTS, dtype=jnp.int32))
    return accumulated.astype(jnp.bfloat16)
```

```python
import functools

import jax
import jax.numpy as jnp
from jax import lax
from jax.experimental import pallas as pl
from jax.experimental.pallas import tpu as pltpu
from jax.sharding import PartitionSpec as P

MESH = pl.DeviceIdType.MESH
BF16 = jnp.bfloat16
F32 = jnp.float32
LINE = 4
SIDES = 2


def slot_cap(row_count, top_count, expert_count):
    return max(2, row_count * top_count * 5 // (2 * expert_count))


def slot_positions(block_ids, expert_count, cap):
    one_hot = (block_ids[..., None] == jnp.arange(expert_count, dtype=jnp.int32)).astype(jnp.int32)
    flattened = one_hot.reshape(-1, expert_count)
    preceding = jnp.cumsum(flattened, axis=0) - flattened
    position = jnp.sum(preceding * flattened, axis=1).reshape(block_ids.shape)
    return block_ids * cap + position


def general(tokens, expert_ids, route_weights, gate_weight, up_weight, down_weight):
    row_count, model_width = tokens.shape
    top_count = expert_ids.shape[1]
    expert_count = lax.axis_size("local")
    cap = slot_cap(row_count, top_count, expert_count)
    home_slot = slot_positions(expert_ids, expert_count, cap)
    outgoing = jnp.zeros((expert_count * cap, model_width), BF16)
    outgoing = outgoing.at[home_slot.reshape(-1)].set(jnp.repeat(tokens, top_count, axis=0))
    gate = lax.all_gather(gate_weight[0], "node", axis=1, tiled=True)
    up = lax.all_gather(up_weight[0], "node", axis=1, tiled=True)
    down = lax.all_gather(down_weight[0], "node", axis=0, tiled=True)
    received = lax.all_to_all(
        outgoing.reshape(expert_count, cap, model_width), "local", split_axis=0, concat_axis=0, tiled=True
    ).reshape(expert_count * cap, model_width)
    gate_act = jnp.dot(received, gate, preferred_element_type=F32)
    up_act = jnp.dot(received, up, preferred_element_type=F32)
    hidden = (jax.nn.silu(gate_act) * up_act).astype(BF16)
    finished = jnp.dot(hidden, down, preferred_element_type=F32).astype(BF16)
    returned = lax.all_to_all(
        finished.reshape(expert_count, cap, model_width), "local", split_axis=0, concat_axis=0, tiled=True
    )
    gathered_out = returned.reshape(expert_count * cap, model_width)[home_slot.reshape(-1)]
    gathered_out = gathered_out.reshape(row_count, top_count, model_width)
    return jnp.sum(route_weights[..., None] * gathered_out.astype(F32), axis=1).astype(BF16)


def layer_kernel(
    cap, tile, tokens, meta, gate_w, up_w, down_w, out,
    X, M, WG, WU, WD, CIN, CSEND, HID, EOUT, RET, D, R,
    load_sem, w_local, w_send, w_recv, x_send, x_recv, m_send, m_recv,
    c_send, c_recv, e_send, e_recv, r_send, r_recv,
):
    me = lax.axis_index("local")
    node = lax.axis_index("node")
    z, y = me // SIDES, me % SIDES
    beside = me + 1 - 2 * y
    last = LINE - 1
    half = z // 2
    mid = (z * (last - z) + 1) // 3
    rows, width = X.shape[1], X.shape[2]
    tiles = width // tile
    experts = lax.axis_size("local")

    def remote(src, dst, send, recv, **where):
        return pltpu.make_async_remote_copy(
            src_ref=src, dst_ref=dst, send_sem=send, recv_sem=recv, device_id=where, device_id_type=MESH
        )

    load = pltpu.make_async_copy(tokens, X.at[z], load_sem)
    load.start()
    own_w = [
        pltpu.make_async_copy(src.at[0], dst.at[0], w_local.at[i])
        for i, (src, dst) in enumerate(((gate_w, WG), (up_w, WU), (down_w, WD)))
    ]
    for copy in own_w:
        copy.start()
    M[z] = meta[...]

    barrier = pltpu.get_barrier_semaphore()
    pl.semaphore_signal(barrier, inc=1, device_id={"node": 1 - node}, device_id_type=MESH)
    pl.semaphore_signal(barrier, inc=1, device_id={"local": beside}, device_id_type=MESH)

    @pl.when(z < last)
    def _():
        pl.semaphore_signal(barrier, inc=1, device_id={"local": me + SIDES}, device_id_type=MESH)

    @pl.when(z > 0)
    def _():
        pl.semaphore_signal(barrier, inc=1, device_id={"local": me - SIDES}, device_id_type=MESH)

    pl.semaphore_wait(barrier, 3 + mid)

    def order(i):
        base = i + mid * (1 - 2 * i) if i < 2 else i
        return base + half * (last - 2 * base)

    def token_copies(o, up):
        where = me + SIDES if up else me - SIDES
        way = 0 if up else 1
        return (
            remote(M.at[o], M.at[o], m_send.at[way, o], m_recv.at[o], local=where),
            remote(X.at[o], X.at[o], x_send.at[way, o], x_recv.at[o], local=where),
        )

    def spread(o, act):
        @pl.when((o <= z) & (z < last))
        def _():
            for copy in token_copies(o, True):
                act(copy)

        @pl.when((o >= z) & (z > 0))
        def _():
            for copy in token_copies(o, False):
                act(copy)

    def compact_copy(o):
        return remote(CSEND.at[o], CIN.at[o, pl.ds(cap, cap)], c_send.at[o], c_recv.at[o], local=beside)

    def result_copy(o):
        return remote(EOUT.at[o, pl.ds(cap, cap)], RET.at[o], e_send.at[o], e_recv.at[o], local=beside)

    def sum_copy(o, way):
        return remote(
            D.at[o], R.at[way, o], r_send.at[o], r_recv.at[way, o], local=me + SIDES * (1 - 2 * way)
        )

    w_remote = [
        remote(src.at[0], dst.at[1], w_send.at[i], w_recv.at[i], node=1 - node)
        for i, (src, dst) in enumerate(((gate_w, WG), (up_w, WU), (down_w, WD)))
    ]

    def place_row(o, e):
        return M[o, pl.ds(e, 1), :]

    def weight_row(o, e):
        return M[o, pl.ds(experts + e, 1), :]

    def to_column(row):
        diagonal = lax.broadcasted_iota(jnp.int32, (rows, rows), 0) == lax.broadcasted_iota(
            jnp.int32, (rows, rows), 1
        )
        return jnp.sum(jnp.where(diagonal, row, 0.0), axis=1, keepdims=True)

    def columns(n):
        return pl.ds(pl.multiple_of(n * tile, tile), tile)

    def stage_a(i):
        o = order(i)
        if i == 0:
            load.wait()
        else:
            for copy in token_copies(o, True):
                copy.wait_recv()
        spread(o, lambda copy: copy.start())
        if i == 0:
            for copy in w_remote:
                copy.start()
        slots = lax.broadcasted_iota(jnp.int32, (cap, rows), 0).astype(F32)
        near = (slots == place_row(o, me)).astype(F32).astype(BF16)
        far = (slots == place_row(o, beside)).astype(F32).astype(BF16)

        def body(n, carry):
            block = X[o, :, columns(n)]
            CSEND[o, :, columns(n)] = jnp.dot(far, block, preferred_element_type=F32).astype(BF16)
            return carry

        lax.fori_loop(0, tiles, body, 0)
        compact_copy(o).start()

        def body(n, carry):
            block = X[o, :, columns(n)]
            CIN[o, 0:cap, columns(n)] = jnp.dot(near, block, preferred_element_type=F32).astype(BF16)
            return carry

        lax.fori_loop(0, tiles, body, 0)

    def stage_b(i):
        o = order(i)
        if i == 0:
            for copy in own_w:
                copy.wait()
            for copy in w_remote:
                copy.wait_recv()
        compact_copy(o).wait_recv()
        part = WG.shape[2] // 2

        def body(t, carry):
            cols = pl.ds(pl.multiple_of((t % 2) * part, part), part)
            gate_act = jnp.dot(CIN[o], WG[t // 2, :, cols], preferred_element_type=F32)
            up_act = jnp.dot(CIN[o], WU[t // 2, :, cols], preferred_element_type=F32)
            hidden = gate_act / (1.0 + jnp.exp(-gate_act)) * up_act
            HID[:, pl.ds(pl.multiple_of(t * part, part), part)] = hidden.astype(BF16)
            return carry

        lax.fori_loop(0, 4, body, 0)

        def body(n, carry):
            total = jnp.dot(HID[:, : 2 * part], WD[0, :, columns(n)], preferred_element_type=F32)
            total += jnp.dot(HID[:, 2 * part :], WD[1, :, columns(n)], preferred_element_type=F32)
            EOUT[o, :, columns(n)] = total.astype(BF16)
            return carry

        lax.fori_loop(0, tiles, body, 0)
        result_copy(o).start()

    def stage_c(i):
        o = order(i)
        slots = lax.broadcasted_iota(jnp.int32, (rows, cap), 1).astype(F32)
        near = (slots == to_column(place_row(o, me))).astype(F32).astype(BF16)
        far = (slots == to_column(place_row(o, beside))).astype(F32).astype(BF16)
        near_w, far_w = to_column(weight_row(o, me)), to_column(weight_row(o, beside))
        result_copy(o).wait_recv()

        def body(n, carry):
            a = jnp.dot(near, EOUT[o, 0:cap, columns(n)], preferred_element_type=F32)
            b = jnp.dot(far, RET[o, :, columns(n)], preferred_element_type=F32)
            D[o, :, columns(n)] = (near_w * a + far_w * b).astype(BF16)
            return carry

        lax.fori_loop(0, tiles, body, 0)
        if i > 0:
            @pl.when(mid == 0)
            def _():
                sum_copy(o, half).start()

    stage_a(0)
    stage_a(1)
    stage_b(0)
    stage_a(2)

    @pl.when(mid == 1)
    def _():
        stage_a(3)

    stage_b(1)
    stage_c(0)

    @pl.when(mid == 0)
    def _():
        stage_a(3)

    stage_b(2)
    stage_c(1)
    stage_b(3)
    stage_c(2)
    stage_c(3)

    @pl.when(mid == 1)
    def _():
        for base, way in ((2, half), (3, half), (0, 1 - half)):
            o = base + half * (last - 2 * base)
            copy = sum_copy(o, way)
            copy.wait_recv()

            def body(n, carry):
                total = D[o, :, columns(n)].astype(F32) + R[way, o, :, columns(n)].astype(F32)
                D[o, :, columns(n)] = total.astype(BF16)
                return carry

            lax.fori_loop(0, tiles, body, 0)
            copy.start()

    def body(n, carry):
        out[:, columns(n)] = D[z, :, columns(n)]
        return carry

    lax.fori_loop(0, tiles, body, 0)

    def add_in(way):
        sum_copy(z, way).wait_recv()

        def body(n, carry):
            total = out[:, columns(n)].astype(F32) + R[way, z, :, columns(n)].astype(F32)
            out[:, columns(n)] = total.astype(BF16)
            return carry

        lax.fori_loop(0, tiles, body, 0)

    @pl.when(z > 0)
    def _():
        add_in(0)

    @pl.when(z < last)
    def _():
        add_in(1)

    for copy in w_remote:
        copy.wait_send()
    for i in range(LINE):
        o = order(i)
        spread(o, lambda copy: copy.wait_send())
        compact_copy(o).wait_send()
        result_copy(o).wait_send()
        if i > 0:
            sum_copy(o, half).wait_send()


def paired(tokens, expert_ids, route_weights, gate_weight, up_weight, down_weight):
    rows, width = tokens.shape
    top_count = expert_ids.shape[1]
    experts = lax.axis_size("local")
    cap = slot_cap(rows, top_count, experts)
    hidden = gate_weight.shape[2]
    named = expert_ids.T[:, None, :] == jnp.arange(experts, dtype=jnp.int32)[None, :, None]
    chosen = jnp.any(named, axis=0)
    place = jnp.cumsum(chosen.astype(F32), axis=1) - 1.0
    place = jnp.where(chosen, place, -1.0)
    weight = jnp.sum(jnp.where(named, route_weights.T[:, None, :], 0.0), axis=0)
    meta = jnp.concatenate([place, weight], axis=0)
    tile = 512 if width % 512 == 0 else 128
    dma = pltpu.SemaphoreType.DMA
    return pl.pallas_call(
        functools.partial(layer_kernel, cap, tile),
        out_shape=jax.ShapeDtypeStruct((rows, width), BF16),
        in_specs=[
            pl.BlockSpec(memory_space=pl.ANY),
            pl.BlockSpec(memory_space=pltpu.VMEM),
            pl.BlockSpec(memory_space=pl.ANY),
            pl.BlockSpec(memory_space=pl.ANY),
            pl.BlockSpec(memory_space=pl.ANY),
        ],
        out_specs=pl.BlockSpec(memory_space=pltpu.VMEM),
        scratch_shapes=[
            pltpu.VMEM((LINE, rows, width), BF16),
            pltpu.VMEM((LINE, 2 * experts, rows), F32),
            pltpu.VMEM((2, width, hidden), BF16),
            pltpu.VMEM((2, width, hidden), BF16),
            pltpu.VMEM((2, hidden, width), BF16),
            pltpu.VMEM((LINE, 2 * cap, width), BF16),
            pltpu.VMEM((LINE, cap, width), BF16),
            pltpu.VMEM((2 * cap, 2 * hidden), BF16),
            pltpu.VMEM((LINE, 2 * cap, width), BF16),
            pltpu.VMEM((LINE, cap, width), BF16),
            pltpu.VMEM((LINE, rows, width), BF16),
            pltpu.VMEM((2, LINE, rows, width), BF16),
            dma, dma((3,)), dma((3,)), dma((3,)),
            dma((2, LINE)), dma((LINE,)), dma((2, LINE)), dma((LINE,)),
            dma((LINE,)), dma((LINE,)), dma((LINE,)), dma((LINE,)),
            dma((LINE,)), dma((2, LINE)),
        ],
        compiler_params=pltpu.CompilerParams(
            collective_id=0, has_side_effects=True, vmem_limit_bytes=60 * 1024 * 1024
        ),
        cost_estimate=pl.CostEstimate(
            flops=12 * LINE * cap * width * 2 * hidden,
            bytes_accessed=12 * width * hidden,
            transcendentals=4 * LINE * cap * hidden,
        ),
    )(tokens, meta, gate_weight, up_weight, down_weight)


def solution(mesh):
    placed = (
        P(("rep", "node", "local"), None),
        P(("rep", "node", "local"), None),
        P(("rep", "node", "local"), None),
        P("local", None, "node"),
        P("local", None, "node"),
        P("local", "node", None),
    )
    small = mesh.shape["local"] == LINE * SIDES and mesh.shape["node"] == 2
    return jax.shard_map(
        paired if small else general,
        mesh=mesh,
        in_specs=placed,
        out_specs=P(("rep", "node", "local"), None),
        check_vma=False,
    )
```

```python
import functools

import jax
import jax.numpy as jnp
from jax import lax
from jax.experimental import pallas as pl
from jax.experimental.pallas import tpu as pltpu
from jax.sharding import PartitionSpec as P

MESH = pl.DeviceIdType.MESH
BF16 = jnp.bfloat16
F32 = jnp.float32
LINE = 4
SIDES = 2


def slot_cap(row_count, top_count, expert_count):
    return max(2, row_count * top_count * 5 // (2 * expert_count))


def slot_positions(block_ids, expert_count, cap):
    one_hot = (block_ids[..., None] == jnp.arange(expert_count, dtype=jnp.int32)).astype(jnp.int32)
    flattened = one_hot.reshape(-1, expert_count)
    preceding = jnp.cumsum(flattened, axis=0) - flattened
    position = jnp.sum(preceding * flattened, axis=1).reshape(block_ids.shape)
    return block_ids * cap + position


def general(tokens, expert_ids, route_weights, gate_weight, up_weight, down_weight):
    row_count, model_width = tokens.shape
    top_count = expert_ids.shape[1]
    expert_count = lax.axis_size("local")
    cap = slot_cap(row_count, top_count, expert_count)
    home_slot = slot_positions(expert_ids, expert_count, cap)
    outgoing = jnp.zeros((expert_count * cap, model_width), BF16)
    outgoing = outgoing.at[home_slot.reshape(-1)].set(jnp.repeat(tokens, top_count, axis=0))
    gate = lax.all_gather(gate_weight[0], "node", axis=1, tiled=True)
    up = lax.all_gather(up_weight[0], "node", axis=1, tiled=True)
    down = lax.all_gather(down_weight[0], "node", axis=0, tiled=True)
    received = lax.all_to_all(
        outgoing.reshape(expert_count, cap, model_width), "local", split_axis=0, concat_axis=0, tiled=True
    ).reshape(expert_count * cap, model_width)
    gate_act = jnp.dot(received, gate, preferred_element_type=F32)
    up_act = jnp.dot(received, up, preferred_element_type=F32)
    hidden = (jax.nn.silu(gate_act) * up_act).astype(BF16)
    finished = jnp.dot(hidden, down, preferred_element_type=F32).astype(BF16)
    returned = lax.all_to_all(
        finished.reshape(expert_count, cap, model_width), "local", split_axis=0, concat_axis=0, tiled=True
    )
    gathered_out = returned.reshape(expert_count * cap, model_width)[home_slot.reshape(-1)]
    gathered_out = gathered_out.reshape(row_count, top_count, model_width)
    return jnp.sum(route_weights[..., None] * gathered_out.astype(F32), axis=1).astype(BF16)


def layer_kernel(
    cap, tile, tokens, meta, gate_w, up_w, down_w, out,
    X, M, WG, WU, WD, CIN, CSEND, HID, EOUT, RET, D, R,
    load_sem, w_local, w_send, w_recv, x_send, x_recv, m_send, m_recv,
    c_send, c_recv, e_send, e_recv, r_send, r_recv,
):
    me = lax.axis_index("local")
    node = lax.axis_index("node")
    z, y = me // SIDES, me % SIDES
    beside = me + 1 - 2 * y
    last = LINE - 1
    half = z // 2
    mid = (z * (last - z) + 1) // 3
    rows, width = X.shape[1], X.shape[2]
    tiles = width // tile
    experts = lax.axis_size("local")

    def remote(src, dst, send, recv, **where):
        return pltpu.make_async_remote_copy(
            src_ref=src, dst_ref=dst, send_sem=send, recv_sem=recv, device_id=where, device_id_type=MESH
        )

    load = pltpu.make_async_copy(tokens, X.at[z], load_sem)
    load.start()
    own_w = [
        pltpu.make_async_copy(src.at[0], dst.at[0], w_local.at[i])
        for i, (src, dst) in enumerate(((gate_w, WG), (up_w, WU), (down_w, WD)))
    ]
    for copy in own_w:
        copy.start()
    M[z] = meta[...]

    barrier = pltpu.get_barrier_semaphore()
    pl.semaphore_signal(barrier, inc=1, device_id={"node": 1 - node}, device_id_type=MESH)
    pl.semaphore_signal(barrier, inc=1, device_id={"local": beside}, device_id_type=MESH)

    @pl.when(z < last)
    def _():
        pl.semaphore_signal(barrier, inc=1, device_id={"local": me + SIDES}, device_id_type=MESH)

    @pl.when(z > 0)
    def _():
        pl.semaphore_signal(barrier, inc=1, device_id={"local": me - SIDES}, device_id_type=MESH)

    pl.semaphore_wait(barrier, 3 + mid)

    def order(i):
        base = i + mid * (1 - 2 * i) if i < 2 else i
        return base + half * (last - 2 * base)

    def columns(n):
        return pl.ds(pl.multiple_of(n * tile, tile), tile)

    def place_copy(o, up):
        where = me + SIDES if up else me - SIDES
        return remote(M.at[o], M.at[o], m_send.at[0 if up else 1, o], m_recv.at[o], local=where)

    def token_copy(o, n, up):
        where = me + SIDES if up else me - SIDES
        block = X.at[o, :, columns(n)]
        return remote(block, block, x_send.at[0 if up else 1, o, n], x_recv.at[o, n], local=where)

    def spread(o, act):
        @pl.when((o <= z) & (z < last))
        def _():
            act(True)

        @pl.when((o >= z) & (z > 0))
        def _():
            act(False)

    def compact_copy(o, n):
        block = CIN.at[o, pl.ds(cap, cap), columns(n)]
        return remote(CSEND.at[o, :, columns(n)], block, c_send.at[o, n], c_recv.at[o, n], local=beside)

    def result_copy(o, n):
        block = EOUT.at[o, pl.ds(cap, cap), columns(n)]
        return remote(block, RET.at[o, :, columns(n)], e_send.at[o, n], e_recv.at[o, n], local=beside)

    def sum_copy(o, n, way):
        where = me + SIDES * (1 - 2 * way)
        block = D.at[o, :, columns(n)]
        return remote(block, R.at[way, o, :, columns(n)], r_send.at[o, n], r_recv.at[way, o, n], local=where)

    def each(body):
        def step(n, carry):
            body(n)
            return carry

        lax.fori_loop(0, tiles, step, 0)

    w_remote = [
        remote(src.at[0], dst.at[1], w_send.at[i], w_recv.at[i], node=1 - node)
        for i, (src, dst) in enumerate(((gate_w, WG), (up_w, WU), (down_w, WD)))
    ]

    def place_row(o, e):
        return M[o, pl.ds(e, 1), :]

    def weight_row(o, e):
        return M[o, pl.ds(experts + e, 1), :]

    def to_column(row):
        diagonal = lax.broadcasted_iota(jnp.int32, (rows, rows), 0) == lax.broadcasted_iota(
            jnp.int32, (rows, rows), 1
        )
        return jnp.sum(jnp.where(diagonal, row, 0.0), axis=1, keepdims=True)

    def stage_a(i):
        o = order(i)
        if i == 0:
            load.wait()
        else:
            place_copy(o, True).wait_recv()
        spread(o, lambda up: place_copy(o, up).start())
        slots = lax.broadcasted_iota(jnp.int32, (cap, rows), 0).astype(F32)
        near = (slots == place_row(o, me)).astype(F32).astype(BF16)
        far = (slots == place_row(o, beside)).astype(F32).astype(BF16)

        @each
        def _(n):
            if i > 0:
                token_copy(o, n, True).wait_recv()
            spread(o, lambda up: token_copy(o, n, up).start())
            block = X[o, :, columns(n)]
            CSEND[o, :, columns(n)] = jnp.dot(far, block, preferred_element_type=F32).astype(BF16)
            compact_copy(o, n).start()
            CIN[o, 0:cap, columns(n)] = jnp.dot(near, block, preferred_element_type=F32).astype(BF16)

        if i == 0:
            for copy in w_remote:
                copy.start()

    def stage_b(i):
        o = order(i)
        if i == 0:
            for copy in own_w:
                copy.wait()
            for copy in w_remote:
                copy.wait_recv()
        each(lambda n: compact_copy(o, n).wait_recv())
        part = WG.shape[2] // 2

        def body(t, carry):
            cols = pl.ds(pl.multiple_of((t % 2) * part, part), part)
            gate_act = jnp.dot(CIN[o], WG[t // 2, :, cols], preferred_element_type=F32)
            up_act = jnp.dot(CIN[o], WU[t // 2, :, cols], preferred_element_type=F32)
            hidden = gate_act / (1.0 + jnp.exp(-gate_act)) * up_act
            HID[:, pl.ds(pl.multiple_of(t * part, part), part)] = hidden.astype(BF16)
            return carry

        lax.fori_loop(0, 4, body, 0)

        @each
        def _(n):
            total = jnp.dot(HID[:, : 2 * part], WD[0, :, columns(n)], preferred_element_type=F32)
            total += jnp.dot(HID[:, 2 * part :], WD[1, :, columns(n)], preferred_element_type=F32)
            EOUT[o, :, columns(n)] = total.astype(BF16)
            result_copy(o, n).start()

    def stage_c(i):
        o = order(i)
        slots = lax.broadcasted_iota(jnp.int32, (rows, cap), 1).astype(F32)
        near = (slots == to_column(place_row(o, me))).astype(F32).astype(BF16)
        far = (slots == to_column(place_row(o, beside))).astype(F32).astype(BF16)
        near_w, far_w = to_column(weight_row(o, me)), to_column(weight_row(o, beside))

        @each
        def _(n):
            result_copy(o, n).wait_recv()
            a = jnp.dot(near, EOUT[o, 0:cap, columns(n)], preferred_element_type=F32)
            b = jnp.dot(far, RET[o, :, columns(n)], preferred_element_type=F32)
            D[o, :, columns(n)] = (near_w * a + far_w * b).astype(BF16)
            if i > 0:
                @pl.when(mid == 0)
                def _():
                    sum_copy(o, n, half).start()

    stage_a(0)
    stage_a(1)
    stage_b(0)
    stage_a(2)

    @pl.when(mid == 1)
    def _():
        stage_a(3)

    stage_b(1)
    stage_c(0)

    @pl.when(mid == 0)
    def _():
        stage_a(3)

    stage_b(2)
    stage_c(1)
    stage_b(3)
    stage_c(2)
    stage_c(3)

    def pass_on(base, way, n):
        o = base + half * (last - 2 * base)
        copy = sum_copy(o, n, way)
        copy.wait_recv()
        total = D[o, :, columns(n)].astype(F32) + R[way, o, :, columns(n)].astype(F32)
        D[o, :, columns(n)] = total.astype(BF16)
        copy.start()

    @pl.when(mid == 1)
    def _():
        each(lambda n: pass_on(2, half, n))

        @each
        def _(n):
            pass_on(3, half, n)
            pass_on(0, 1 - half, n)

    @pl.when(mid == 1)
    def _():
        @each
        def _(n):
            sum_copy(z, n, half).wait_recv()
            sum_copy(z, n, 1 - half).wait_recv()
            total = D[z, :, columns(n)].astype(F32) + R[0, z, :, columns(n)].astype(F32)
            total += R[1, z, :, columns(n)].astype(F32)
            out[:, columns(n)] = total.astype(BF16)

    @pl.when(mid == 0)
    def _():
        @each
        def _(n):
            sum_copy(z, n, 1 - half).wait_recv()
            total = D[z, :, columns(n)].astype(F32) + R[1 - half, z, :, columns(n)].astype(F32)
            out[:, columns(n)] = total.astype(BF16)

    for copy in w_remote:
        copy.wait_send()
    for i in range(LINE):
        o = order(i)
        spread(o, lambda up: place_copy(o, up).wait_send())

        @each
        def _(n):
            spread(o, lambda up: token_copy(o, n, up).wait_send())
            compact_copy(o, n).wait_send()
            result_copy(o, n).wait_send()
            if i > 0:
                sum_copy(o, n, half).wait_send()


def paired(tokens, expert_ids, route_weights, gate_weight, up_weight, down_weight):
    rows, width = tokens.shape
    top_count = expert_ids.shape[1]
    experts = lax.axis_size("local")
    cap = slot_cap(rows, top_count, experts)
    hidden = gate_weight.shape[2]
    named = expert_ids.T[:, None, :] == jnp.arange(experts, dtype=jnp.int32)[None, :, None]
    chosen = jnp.any(named, axis=0)
    place = jnp.cumsum(chosen.astype(F32), axis=1) - 1.0
    place = jnp.where(chosen, place, -1.0)
    weight = jnp.sum(jnp.where(named, route_weights.T[:, None, :], 0.0), axis=0)
    meta = jnp.concatenate([place, weight], axis=0)
    tile = 512 if width % 512 == 0 else 128
    tiles = width // tile
    dma = pltpu.SemaphoreType.DMA
    return pl.pallas_call(
        functools.partial(layer_kernel, cap, tile),
        out_shape=jax.ShapeDtypeStruct((rows, width), BF16),
        in_specs=[
            pl.BlockSpec(memory_space=pl.ANY),
            pl.BlockSpec(memory_space=pltpu.VMEM),
            pl.BlockSpec(memory_space=pl.ANY),
            pl.BlockSpec(memory_space=pl.ANY),
            pl.BlockSpec(memory_space=pl.ANY),
        ],
        out_specs=pl.BlockSpec(memory_space=pltpu.VMEM),
        scratch_shapes=[
            pltpu.VMEM((LINE, rows, width), BF16),
            pltpu.VMEM((LINE, 2 * experts, rows), F32),
            pltpu.VMEM((2, width, hidden), BF16),
            pltpu.VMEM((2, width, hidden), BF16),
            pltpu.VMEM((2, hidden, width), BF16),
            pltpu.VMEM((LINE, 2 * cap, width), BF16),
            pltpu.VMEM((LINE, cap, width), BF16),
            pltpu.VMEM((2 * cap, 2 * hidden), BF16),
            pltpu.VMEM((LINE, 2 * cap, width), BF16),
            pltpu.VMEM((LINE, cap, width), BF16),
            pltpu.VMEM((LINE, rows, width), BF16),
            pltpu.VMEM((2, LINE, rows, width), BF16),
            dma, dma((3,)), dma((3,)), dma((3,)),
            dma((2, LINE, tiles)), dma((LINE, tiles)), dma((2, LINE)), dma((LINE,)),
            dma((LINE, tiles)), dma((LINE, tiles)), dma((LINE, tiles)), dma((LINE, tiles)),
            dma((LINE, tiles)), dma((2, LINE, tiles)),
        ],
        compiler_params=pltpu.CompilerParams(
            collective_id=0, has_side_effects=True, vmem_limit_bytes=60 * 1024 * 1024
        ),
        cost_estimate=pl.CostEstimate(
            flops=12 * LINE * cap * width * 2 * hidden,
            bytes_accessed=12 * width * hidden,
            transcendentals=4 * LINE * cap * hidden,
        ),
    )(tokens, meta, gate_weight, up_weight, down_weight)


def solution(mesh):
    placed = (
        P(("rep", "node", "local"), None),
        P(("rep", "node", "local"), None),
        P(("rep", "node", "local"), None),
        P("local", None, "node"),
        P("local", None, "node"),
        P("local", "node", None),
    )
    small = mesh.shape["local"] == LINE * SIDES and mesh.shape["node"] == 2
    return jax.shard_map(
        paired if small else general,
        mesh=mesh,
        in_specs=placed,
        out_specs=P(("rep", "node", "local"), None),
        check_vma=False,
    )
```

```python
import functools

import jax
import jax.numpy as jnp
from jax import lax
from jax.experimental import pallas as pl
from jax.experimental.pallas import tpu as pltpu
from jax.sharding import PartitionSpec as P

MESH = pl.DeviceIdType.MESH
BF16 = jnp.bfloat16
F32 = jnp.float32
LINE = 4
SIDES = 2


def slot_cap(row_count, top_count, expert_count):
    return max(2, row_count * top_count * 5 // (2 * expert_count))


def slot_positions(block_ids, expert_count, cap):
    one_hot = (block_ids[..., None] == jnp.arange(expert_count, dtype=jnp.int32)).astype(jnp.int32)
    flattened = one_hot.reshape(-1, expert_count)
    preceding = jnp.cumsum(flattened, axis=0) - flattened
    position = jnp.sum(preceding * flattened, axis=1).reshape(block_ids.shape)
    return block_ids * cap + position


def general(tokens, expert_ids, route_weights, gate_weight, up_weight, down_weight):
    row_count, model_width = tokens.shape
    top_count = expert_ids.shape[1]
    expert_count = lax.axis_size("local")
    cap = slot_cap(row_count, top_count, expert_count)
    home_slot = slot_positions(expert_ids, expert_count, cap)
    outgoing = jnp.zeros((expert_count * cap, model_width), BF16)
    outgoing = outgoing.at[home_slot.reshape(-1)].set(jnp.repeat(tokens, top_count, axis=0))
    gate = lax.all_gather(gate_weight[0], "node", axis=1, tiled=True)
    up = lax.all_gather(up_weight[0], "node", axis=1, tiled=True)
    down = lax.all_gather(down_weight[0], "node", axis=0, tiled=True)
    received = lax.all_to_all(
        outgoing.reshape(expert_count, cap, model_width), "local", split_axis=0, concat_axis=0, tiled=True
    ).reshape(expert_count * cap, model_width)
    gate_act = jnp.dot(received, gate, preferred_element_type=F32)
    up_act = jnp.dot(received, up, preferred_element_type=F32)
    hidden = (jax.nn.silu(gate_act) * up_act).astype(BF16)
    finished = jnp.dot(hidden, down, preferred_element_type=F32).astype(BF16)
    returned = lax.all_to_all(
        finished.reshape(expert_count, cap, model_width), "local", split_axis=0, concat_axis=0, tiled=True
    )
    gathered_out = returned.reshape(expert_count * cap, model_width)[home_slot.reshape(-1)]
    gathered_out = gathered_out.reshape(row_count, top_count, model_width)
    return jnp.sum(route_weights[..., None] * gathered_out.astype(F32), axis=1).astype(BF16)


def layer_kernel(
    cap, tile, tokens, meta, gate_w, up_w, down_w, out,
    X, M, WG, WU, WD, CIN, CSEND, HID, EOUT, RET, D, R,
    load_sem, w_local, w_send, w_recv, x_send, x_recv, m_send, m_recv,
    c_send, c_recv, e_send, e_recv, r_send, r_recv,
):
    me = lax.axis_index("local")
    node = lax.axis_index("node")
    z, y = me // SIDES, me % SIDES
    beside = me + 1 - 2 * y
    last = LINE - 1
    half = z // 2
    mid = (z * (last - z) + 1) // 3
    rows, width = X.shape[1], X.shape[2]
    tiles = width // tile
    experts = lax.axis_size("local")

    def remote(src, dst, send, recv, **where):
        return pltpu.make_async_remote_copy(
            src_ref=src, dst_ref=dst, send_sem=send, recv_sem=recv, device_id=where, device_id_type=MESH
        )

    load = pltpu.make_async_copy(tokens, X.at[z], load_sem)
    load.start()
    own_w = [
        pltpu.make_async_copy(src.at[0], dst.at[0], w_local.at[i])
        for i, (src, dst) in enumerate(((gate_w, WG), (up_w, WU), (down_w, WD)))
    ]
    for copy in own_w:
        copy.start()
    M[z] = meta[...]

    barrier = pltpu.get_barrier_semaphore()
    pl.semaphore_signal(barrier, inc=1, device_id={"node": 1 - node}, device_id_type=MESH)
    pl.semaphore_signal(barrier, inc=1, device_id={"local": beside}, device_id_type=MESH)

    @pl.when(z < last)
    def _():
        pl.semaphore_signal(barrier, inc=1, device_id={"local": me + SIDES}, device_id_type=MESH)

    @pl.when(z > 0)
    def _():
        pl.semaphore_signal(barrier, inc=1, device_id={"local": me - SIDES}, device_id_type=MESH)

    pl.semaphore_wait(barrier, 3 + mid)

    def order(i):
        base = i + mid * (1 - 2 * i) if i < 2 else i
        return base + half * (last - 2 * base)

    def columns(n):
        return pl.ds(pl.multiple_of(n * tile, tile), tile)

    def place_copy(o, up):
        where = me + SIDES if up else me - SIDES
        return remote(M.at[o], M.at[o], m_send.at[0 if up else 1, o], m_recv.at[o], local=where)

    def token_copy(o, n, up):
        where = me + SIDES if up else me - SIDES
        block = X.at[o, :, columns(n)]
        return remote(block, block, x_send.at[0 if up else 1, o, n], x_recv.at[o, n], local=where)

    def spread(o, act):
        @pl.when((o <= z) & (z < last))
        def _():
            act(True)

        @pl.when((o >= z) & (z > 0))
        def _():
            act(False)

    def compact_copy(o, n):
        block = CIN.at[o, pl.ds(cap, cap), columns(n)]
        return remote(CSEND.at[o, :, columns(n)], block, c_send.at[o, n], c_recv.at[o, n], local=beside)

    def result_copy(o, n):
        block = EOUT.at[o, pl.ds(cap, cap), columns(n)]
        return remote(block, RET.at[o, :, columns(n)], e_send.at[o, n], e_recv.at[o, n], local=beside)

    def sum_copy(o, n, way):
        where = me + SIDES * (1 - 2 * way)
        block = D.at[o, :, columns(n)]
        return remote(block, R.at[way, o, :, columns(n)], r_send.at[o, n], r_recv.at[way, o, n], local=where)

    def each(body):
        def step(n, carry):
            body(n)
            return carry

        lax.fori_loop(0, tiles, step, 0)

    w_remote = [
        remote(src.at[0], dst.at[1], w_send.at[i], w_recv.at[i], node=1 - node)
        for i, (src, dst) in enumerate(((gate_w, WG), (up_w, WU), (down_w, WD)))
    ]

    def place_row(o, e):
        return M[o, pl.ds(e, 1), :]

    def weight_row(o, e):
        return M[o, pl.ds(experts + e, 1), :]

    def to_column(row):
        diagonal = lax.broadcasted_iota(jnp.int32, (rows, rows), 0) == lax.broadcasted_iota(
            jnp.int32, (rows, rows), 1
        )
        return jnp.sum(jnp.where(diagonal, row, 0.0), axis=1, keepdims=True)

    def stage_a(i):
        o = order(i)
        if i == 0:
            load.wait()
        else:
            place_copy(o, True).wait_recv()
        spread(o, lambda up: place_copy(o, up).start())
        slots = lax.broadcasted_iota(jnp.int32, (cap, rows), 0).astype(F32)
        near = (slots == place_row(o, me)).astype(F32).astype(BF16)
        far = (slots == place_row(o, beside)).astype(F32).astype(BF16)

        @each
        def _(n):
            if i > 0:
                token_copy(o, n, True).wait_recv()
            spread(o, lambda up: token_copy(o, n, up).start())
            block = X[o, :, columns(n)]
            CSEND[o, :, columns(n)] = jnp.dot(far, block, preferred_element_type=F32).astype(BF16)
            compact_copy(o, n).start()
            CIN[o, 0:cap, columns(n)] = jnp.dot(near, block, preferred_element_type=F32).astype(BF16)

        if i == 0:
            for copy in w_remote:
                copy.start()

    def stage_b(i):
        o = order(i)
        each(lambda n: compact_copy(o, n).wait_recv())
        part = WG.shape[2] // 2

        def body(t, carry):
            cols = pl.ds(pl.multiple_of((t % 2) * part, part), part)
            gate_act = jnp.dot(CIN[o], WG[t // 2, :, cols], preferred_element_type=F32)
            up_act = jnp.dot(CIN[o], WU[t // 2, :, cols], preferred_element_type=F32)
            hidden = gate_act / (1.0 + jnp.exp(-gate_act)) * up_act
            HID[:, pl.ds(pl.multiple_of(t * part, part), part)] = hidden.astype(BF16)
            return carry

        lax.fori_loop(0, 4, body, 0)

        @each
        def _(n):
            total = jnp.dot(HID[:, : 2 * part], WD[0, :, columns(n)], preferred_element_type=F32)
            total += jnp.dot(HID[:, 2 * part :], WD[1, :, columns(n)], preferred_element_type=F32)
            EOUT[o, :, columns(n)] = total.astype(BF16)
            result_copy(o, n).start()

    def stage_c(i, send):
        o = order(i)
        slots = lax.broadcasted_iota(jnp.int32, (rows, cap), 1).astype(F32)
        near = (slots == to_column(place_row(o, me))).astype(F32).astype(BF16)
        far = (slots == to_column(place_row(o, beside))).astype(F32).astype(BF16)
        near_w, far_w = to_column(weight_row(o, me)), to_column(weight_row(o, beside))

        @each
        def _(n):
            result_copy(o, n).wait_recv()
            a = jnp.dot(near, EOUT[o, 0:cap, columns(n)], preferred_element_type=F32)
            b = jnp.dot(far, RET[o, :, columns(n)], preferred_element_type=F32)
            D[o, :, columns(n)] = (near_w * a + far_w * b).astype(BF16)
            if send:
                sum_copy(o, n, half).start()

    def pass_on(base, way, n):
        o = base + half * (last - 2 * base)
        copy = sum_copy(o, n, way)
        copy.wait_recv()
        total = D[o, :, columns(n)].astype(F32) + R[way, o, :, columns(n)].astype(F32)
        D[o, :, columns(n)] = total.astype(BF16)
        copy.start()

    stage_a(0)
    stage_a(1)
    for copy in own_w:
        copy.wait()
    for copy in w_remote:
        copy.wait_recv()

    @pl.when(mid == 1)
    def _():
        stage_a(2)
        stage_a(3)
        for i in (2, 3, 1, 0):
            stage_b(i)
        stage_c(2, False)
        each(lambda n: pass_on(2, half, n))
        stage_c(3, False)
        stage_c(1, False)

        @each
        def _(n):
            pass_on(3, half, n)
            pass_on(0, 1 - half, n)

        stage_c(0, False)

    @pl.when(mid == 0)
    def _():
        stage_b(1)
        stage_c(1, True)
        stage_a(2)
        stage_b(2)
        stage_c(2, True)
        stage_a(3)
        stage_b(3)
        stage_b(0)
        stage_c(3, True)
        stage_c(0, False)

    @pl.when(mid == 1)
    def _():
        @each
        def _(n):
            sum_copy(z, n, half).wait_recv()
            sum_copy(z, n, 1 - half).wait_recv()
            total = D[z, :, columns(n)].astype(F32) + R[0, z, :, columns(n)].astype(F32)
            total += R[1, z, :, columns(n)].astype(F32)
            out[:, columns(n)] = total.astype(BF16)

    @pl.when(mid == 0)
    def _():
        @each
        def _(n):
            sum_copy(z, n, 1 - half).wait_recv()
            total = D[z, :, columns(n)].astype(F32) + R[1 - half, z, :, columns(n)].astype(F32)
            out[:, columns(n)] = total.astype(BF16)

    for copy in w_remote:
        copy.wait_send()
    for i in range(LINE):
        o = order(i)
        spread(o, lambda up: place_copy(o, up).wait_send())

        @each
        def _(n):
            spread(o, lambda up: token_copy(o, n, up).wait_send())
            compact_copy(o, n).wait_send()
            result_copy(o, n).wait_send()
            if i > 0:
                sum_copy(o, n, half).wait_send()


def paired(tokens, expert_ids, route_weights, gate_weight, up_weight, down_weight):
    rows, width = tokens.shape
    top_count = expert_ids.shape[1]
    experts = lax.axis_size("local")
    cap = slot_cap(rows, top_count, experts)
    hidden = gate_weight.shape[2]
    named = expert_ids.T[:, None, :] == jnp.arange(experts, dtype=jnp.int32)[None, :, None]
    chosen = jnp.any(named, axis=0)
    place = jnp.cumsum(chosen.astype(F32), axis=1) - 1.0
    place = jnp.where(chosen, place, -1.0)
    weight = jnp.sum(jnp.where(named, route_weights.T[:, None, :], 0.0), axis=0)
    meta = jnp.concatenate([place, weight], axis=0)
    tile = 512 if width % 512 == 0 else 128
    tiles = width // tile
    dma = pltpu.SemaphoreType.DMA
    return pl.pallas_call(
        functools.partial(layer_kernel, cap, tile),
        out_shape=jax.ShapeDtypeStruct((rows, width), BF16),
        in_specs=[
            pl.BlockSpec(memory_space=pl.ANY),
            pl.BlockSpec(memory_space=pltpu.VMEM),
            pl.BlockSpec(memory_space=pl.ANY),
            pl.BlockSpec(memory_space=pl.ANY),
            pl.BlockSpec(memory_space=pl.ANY),
        ],
        out_specs=pl.BlockSpec(memory_space=pltpu.VMEM),
        scratch_shapes=[
            pltpu.VMEM((LINE, rows, width), BF16),
            pltpu.VMEM((LINE, 2 * experts, rows), F32),
            pltpu.VMEM((2, width, hidden), BF16),
            pltpu.VMEM((2, width, hidden), BF16),
            pltpu.VMEM((2, hidden, width), BF16),
            pltpu.VMEM((LINE, 2 * cap, width), BF16),
            pltpu.VMEM((LINE, cap, width), BF16),
            pltpu.VMEM((2 * cap, 2 * hidden), BF16),
            pltpu.VMEM((LINE, 2 * cap, width), BF16),
            pltpu.VMEM((LINE, cap, width), BF16),
            pltpu.VMEM((LINE, rows, width), BF16),
            pltpu.VMEM((2, LINE, rows, width), BF16),
            dma, dma((3,)), dma((3,)), dma((3,)),
            dma((2, LINE, tiles)), dma((LINE, tiles)), dma((2, LINE)), dma((LINE,)),
            dma((LINE, tiles)), dma((LINE, tiles)), dma((LINE, tiles)), dma((LINE, tiles)),
            dma((LINE, tiles)), dma((2, LINE, tiles)),
        ],
        compiler_params=pltpu.CompilerParams(
            collective_id=0, has_side_effects=True, vmem_limit_bytes=60 * 1024 * 1024
        ),
        cost_estimate=pl.CostEstimate(
            flops=12 * LINE * cap * width * 2 * hidden,
            bytes_accessed=12 * width * hidden,
            transcendentals=4 * LINE * cap * hidden,
        ),
    )(tokens, meta, gate_weight, up_weight, down_weight)


def solution(mesh):
    placed = (
        P(("rep", "node", "local"), None),
        P(("rep", "node", "local"), None),
        P(("rep", "node", "local"), None),
        P("local", None, "node"),
        P("local", None, "node"),
        P("local", "node", None),
    )
    small = mesh.shape["local"] == LINE * SIDES and mesh.shape["node"] == 2
    return jax.shard_map(
        paired if small else general,
        mesh=mesh,
        in_specs=placed,
        out_specs=P(("rep", "node", "local"), None),
        check_vma=False,
    )
```

```python
import functools

import jax
import jax.numpy as jnp
from jax import lax
from jax.experimental import pallas as pl
from jax.experimental.pallas import tpu as pltpu
from jax.sharding import PartitionSpec as P

MESH = pl.DeviceIdType.MESH
BF16 = jnp.bfloat16
F32 = jnp.float32
LINE = 4
SIDES = 2


def slot_cap(row_count, top_count, expert_count):
    return max(2, row_count * top_count * 5 // (2 * expert_count))


def slot_positions(block_ids, expert_count, cap):
    one_hot = (block_ids[..., None] == jnp.arange(expert_count, dtype=jnp.int32)).astype(jnp.int32)
    flattened = one_hot.reshape(-1, expert_count)
    preceding = jnp.cumsum(flattened, axis=0) - flattened
    position = jnp.sum(preceding * flattened, axis=1).reshape(block_ids.shape)
    return block_ids * cap + position


def general(tokens, expert_ids, route_weights, gate_weight, up_weight, down_weight):
    row_count, model_width = tokens.shape
    top_count = expert_ids.shape[1]
    expert_count = lax.axis_size("local")
    cap = slot_cap(row_count, top_count, expert_count)
    home_slot = slot_positions(expert_ids, expert_count, cap)
    outgoing = jnp.zeros((expert_count * cap, model_width), BF16)
    outgoing = outgoing.at[home_slot.reshape(-1)].set(jnp.repeat(tokens, top_count, axis=0))
    gate = lax.all_gather(gate_weight[0], "node", axis=1, tiled=True)
    up = lax.all_gather(up_weight[0], "node", axis=1, tiled=True)
    down = lax.all_gather(down_weight[0], "node", axis=0, tiled=True)
    received = lax.all_to_all(
        outgoing.reshape(expert_count, cap, model_width), "local", split_axis=0, concat_axis=0, tiled=True
    ).reshape(expert_count * cap, model_width)
    gate_act = jnp.dot(received, gate, preferred_element_type=F32)
    up_act = jnp.dot(received, up, preferred_element_type=F32)
    hidden = (jax.nn.silu(gate_act) * up_act).astype(BF16)
    finished = jnp.dot(hidden, down, preferred_element_type=F32).astype(BF16)
    returned = lax.all_to_all(
        finished.reshape(expert_count, cap, model_width), "local", split_axis=0, concat_axis=0, tiled=True
    )
    gathered_out = returned.reshape(expert_count * cap, model_width)[home_slot.reshape(-1)]
    gathered_out = gathered_out.reshape(row_count, top_count, model_width)
    return jnp.sum(route_weights[..., None] * gathered_out.astype(F32), axis=1).astype(BF16)


def layer_kernel(
    cap, tile, tokens, meta, gate_w, up_w, down_w, out,
    X, M, WG, WU, WD, CIN, CSEND, HID, EOUT, RET, D, R,
    load_sem, w_local, w_send, w_recv, x_send, x_recv, m_send, m_recv,
    c_send, c_recv, e_send, e_recv, r_send, r_recv,
):
    me = lax.axis_index("local")
    node = lax.axis_index("node")
    z, y = me // SIDES, me % SIDES
    beside = me + 1 - 2 * y
    last = LINE - 1
    half = z // 2
    mid = (z * (last - z) + 1) // 3
    rows, width = X.shape[1], X.shape[2]
    tiles = width // tile
    experts = lax.axis_size("local")

    def remote(src, dst, send, recv, **where):
        return pltpu.make_async_remote_copy(
            src_ref=src, dst_ref=dst, send_sem=send, recv_sem=recv, device_id=where, device_id_type=MESH
        )

    load = pltpu.make_async_copy(tokens, X.at[z], load_sem)
    load.start()
    own_w = [
        pltpu.make_async_copy(src.at[0], dst.at[0], w_local.at[i])
        for i, (src, dst) in enumerate(((gate_w, WG), (up_w, WU), (down_w, WD)))
    ]
    for copy in own_w:
        copy.start()
    M[z] = meta[...]

    barrier = pltpu.get_barrier_semaphore()
    pl.semaphore_signal(barrier, inc=1, device_id={"node": 1 - node}, device_id_type=MESH)
    pl.semaphore_signal(barrier, inc=1, device_id={"local": beside}, device_id_type=MESH)

    @pl.when(z < last)
    def _():
        pl.semaphore_signal(barrier, inc=1, device_id={"local": me + SIDES}, device_id_type=MESH)

    @pl.when(z > 0)
    def _():
        pl.semaphore_signal(barrier, inc=1, device_id={"local": me - SIDES}, device_id_type=MESH)

    pl.semaphore_wait(barrier, 3 + mid)

    def order(i):
        base = i + mid * (1 - 2 * i) if i < 2 else i
        return base + half * (last - 2 * base)

    def columns(n):
        return pl.ds(pl.multiple_of(n * tile, tile), tile)

    def place_copy(o, up):
        where = me + SIDES if up else me - SIDES
        return remote(M.at[o], M.at[o], m_send.at[0 if up else 1, o], m_recv.at[o], local=where)

    def token_copy(o, n, up):
        where = me + SIDES if up else me - SIDES
        block = X.at[o, :, columns(n)]
        return remote(block, block, x_send.at[0 if up else 1, o, n], x_recv.at[o, n], local=where)

    def spread(o, act):
        @pl.when((o <= z) & (z < last))
        def _():
            act(True)

        @pl.when((o >= z) & (z > 0))
        def _():
            act(False)

    def compact_copy(o, n):
        block = CIN.at[o, pl.ds(cap, cap), columns(n)]
        return remote(CSEND.at[o, :, columns(n)], block, c_send.at[o, n], c_recv.at[o, n], local=beside)

    def result_copy(o, n):
        block = EOUT.at[o, pl.ds(cap, cap), columns(n)]
        return remote(block, RET.at[o, :, columns(n)], e_send.at[o, n], e_recv.at[o, n], local=beside)

    def sum_copy(o, n, way):
        where = me + SIDES * (1 - 2 * way)
        block = D.at[o, :, columns(n)]
        return remote(block, R.at[way, o, :, columns(n)], r_send.at[o, n], r_recv.at[way, o, n], local=where)

    def each(body):
        def step(n, carry):
            body(n)
            return carry

        lax.fori_loop(0, tiles, step, 0)

    w_remote = [
        remote(src.at[0], dst.at[1], w_send.at[i], w_recv.at[i], node=1 - node)
        for i, (src, dst) in enumerate(((gate_w, WG), (up_w, WU), (down_w, WD)))
    ]

    def place_row(o, e):
        return M[o, pl.ds(e, 1), :]

    def weight_row(o, e):
        return M[o, pl.ds(experts + e, 1), :]

    def to_column(row):
        diagonal = lax.broadcasted_iota(jnp.int32, (rows, rows), 0) == lax.broadcasted_iota(
            jnp.int32, (rows, rows), 1
        )
        return jnp.sum(jnp.where(diagonal, row, 0.0), axis=1, keepdims=True)

    def stage_a(i):
        o = order(i)
        if i == 0:
            load.wait()
        else:
            place_copy(o, True).wait_recv()
        spread(o, lambda up: place_copy(o, up).start())
        slots = lax.broadcasted_iota(jnp.int32, (cap, rows), 0).astype(F32)
        near = (slots == place_row(o, me)).astype(F32).astype(BF16)
        far = (slots == place_row(o, beside)).astype(F32).astype(BF16)

        @each
        def _(n):
            if i > 0:
                token_copy(o, n, True).wait_recv()
            spread(o, lambda up: token_copy(o, n, up).start())
            block = X[o, :, columns(n)]
            CSEND[o, :, columns(n)] = jnp.dot(far, block, preferred_element_type=F32).astype(BF16)
            compact_copy(o, n).start()
            CIN[o, 0:cap, columns(n)] = jnp.dot(near, block, preferred_element_type=F32).astype(BF16)

        if i == 0:
            for copy in w_remote:
                copy.start()

    def stage_b(i):
        o = order(i)
        each(lambda n: compact_copy(o, n).wait_recv())
        part = WG.shape[2] // 2

        def body(t, carry):
            cols = pl.ds(pl.multiple_of((t % 2) * part, part), part)
            gate_act = jnp.dot(CIN[o], WG[t // 2, :, cols], preferred_element_type=F32)
            up_act = jnp.dot(CIN[o], WU[t // 2, :, cols], preferred_element_type=F32)
            hidden = gate_act / (1.0 + jnp.exp(-gate_act)) * up_act
            HID[:, pl.ds(pl.multiple_of(t * part, part), part)] = hidden.astype(BF16)
            return carry

        lax.fori_loop(0, 4, body, 0)

        @each
        def _(n):
            total = jnp.dot(HID[:, : 2 * part], WD[0, :, columns(n)], preferred_element_type=F32)
            total += jnp.dot(HID[:, 2 * part :], WD[1, :, columns(n)], preferred_element_type=F32)
            EOUT[o, :, columns(n)] = total.astype(BF16)
            result_copy(o, n).start()

    def stage_c(i, send):
        o = order(i)
        slots = lax.broadcasted_iota(jnp.int32, (rows, cap), 1).astype(F32)
        near = (slots == to_column(place_row(o, me))).astype(F32).astype(BF16)
        far = (slots == to_column(place_row(o, beside))).astype(F32).astype(BF16)
        near_w, far_w = to_column(weight_row(o, me)), to_column(weight_row(o, beside))

        @each
        def _(n):
            result_copy(o, n).wait_recv()
            a = jnp.dot(near, EOUT[o, 0:cap, columns(n)], preferred_element_type=F32)
            b = jnp.dot(far, RET[o, :, columns(n)], preferred_element_type=F32)
            D[o, :, columns(n)] = (near_w * a + far_w * b).astype(BF16)
            if send:
                sum_copy(o, n, half).start()

    def pass_on(base, way, n):
        o = base + half * (last - 2 * base)
        copy = sum_copy(o, n, way)
        copy.wait_recv()
        total = D[o, :, columns(n)].astype(F32) + R[way, o, :, columns(n)].astype(F32)
        D[o, :, columns(n)] = total.astype(BF16)
        copy.start()

    stage_a(0)
    def weights_here():
        for copy in own_w:
            copy.wait()
        for copy in w_remote:
            copy.wait_recv()

    @pl.when(mid == 1)
    def _():
        stage_a(2)
        stage_a(1)
        stage_a(3)
        weights_here()
        for i in (2, 3, 1, 0):
            stage_b(i)
        stage_c(2, False)
        each(lambda n: pass_on(2, half, n))
        stage_c(3, False)
        stage_c(1, False)

        @each
        def _(n):
            pass_on(3, half, n)
            pass_on(0, 1 - half, n)

        stage_c(0, False)

    @pl.when(mid == 0)
    def _():
        stage_a(1)
        weights_here()
        stage_b(1)
        stage_a(2)
        stage_c(1, True)
        stage_b(2)
        stage_c(2, True)
        stage_a(3)
        stage_b(3)
        stage_b(0)
        stage_c(3, True)
        stage_c(0, False)

    @pl.when(mid == 1)
    def _():
        @each
        def _(n):
            sum_copy(z, n, half).wait_recv()
            sum_copy(z, n, 1 - half).wait_recv()
            total = D[z, :, columns(n)].astype(F32) + R[0, z, :, columns(n)].astype(F32)
            total += R[1, z, :, columns(n)].astype(F32)
            out[:, columns(n)] = total.astype(BF16)

    @pl.when(mid == 0)
    def _():
        @each
        def _(n):
            sum_copy(z, n, 1 - half).wait_recv()
            total = D[z, :, columns(n)].astype(F32) + R[1 - half, z, :, columns(n)].astype(F32)
            out[:, columns(n)] = total.astype(BF16)

    for copy in w_remote:
        copy.wait_send()
    for i in range(LINE):
        o = order(i)
        spread(o, lambda up: place_copy(o, up).wait_send())

        @each
        def _(n):
            spread(o, lambda up: token_copy(o, n, up).wait_send())
            compact_copy(o, n).wait_send()
            result_copy(o, n).wait_send()
            if i > 0:
                sum_copy(o, n, half).wait_send()


def paired(tokens, expert_ids, route_weights, gate_weight, up_weight, down_weight):
    rows, width = tokens.shape
    top_count = expert_ids.shape[1]
    experts = lax.axis_size("local")
    cap = slot_cap(rows, top_count, experts)
    hidden = gate_weight.shape[2]
    named = expert_ids.T[:, None, :] == jnp.arange(experts, dtype=jnp.int32)[None, :, None]
    chosen = jnp.any(named, axis=0)
    place = jnp.cumsum(chosen.astype(F32), axis=1) - 1.0
    place = jnp.where(chosen, place, -1.0)
    weight = jnp.sum(jnp.where(named, route_weights.T[:, None, :], 0.0), axis=0)
    meta = jnp.concatenate([place, weight], axis=0)
    tile = 512 if width % 512 == 0 else 128
    tiles = width // tile
    dma = pltpu.SemaphoreType.DMA
    return pl.pallas_call(
        functools.partial(layer_kernel, cap, tile),
        out_shape=jax.ShapeDtypeStruct((rows, width), BF16),
        in_specs=[
            pl.BlockSpec(memory_space=pl.ANY),
            pl.BlockSpec(memory_space=pltpu.VMEM),
            pl.BlockSpec(memory_space=pl.ANY),
            pl.BlockSpec(memory_space=pl.ANY),
            pl.BlockSpec(memory_space=pl.ANY),
        ],
        out_specs=pl.BlockSpec(memory_space=pltpu.VMEM),
        scratch_shapes=[
            pltpu.VMEM((LINE, rows, width), BF16),
            pltpu.VMEM((LINE, 2 * experts, rows), F32),
            pltpu.VMEM((2, width, hidden), BF16),
            pltpu.VMEM((2, width, hidden), BF16),
            pltpu.VMEM((2, hidden, width), BF16),
            pltpu.VMEM((LINE, 2 * cap, width), BF16),
            pltpu.VMEM((LINE, cap, width), BF16),
            pltpu.VMEM((2 * cap, 2 * hidden), BF16),
            pltpu.VMEM((LINE, 2 * cap, width), BF16),
            pltpu.VMEM((LINE, cap, width), BF16),
            pltpu.VMEM((LINE, rows, width), BF16),
            pltpu.VMEM((2, LINE, rows, width), BF16),
            dma, dma((3,)), dma((3,)), dma((3,)),
            dma((2, LINE, tiles)), dma((LINE, tiles)), dma((2, LINE)), dma((LINE,)),
            dma((LINE, tiles)), dma((LINE, tiles)), dma((LINE, tiles)), dma((LINE, tiles)),
            dma((LINE, tiles)), dma((2, LINE, tiles)),
        ],
        compiler_params=pltpu.CompilerParams(
            collective_id=0, has_side_effects=True, vmem_limit_bytes=60 * 1024 * 1024
        ),
        cost_estimate=pl.CostEstimate(
            flops=12 * LINE * cap * width * 2 * hidden,
            bytes_accessed=12 * width * hidden,
            transcendentals=4 * LINE * cap * hidden,
        ),
    )(tokens, meta, gate_weight, up_weight, down_weight)


def solution(mesh):
    placed = (
        P(("rep", "node", "local"), None),
        P(("rep", "node", "local"), None),
        P(("rep", "node", "local"), None),
        P("local", None, "node"),
        P("local", None, "node"),
        P("local", "node", None),
    )
    small = mesh.shape["local"] == LINE * SIDES and mesh.shape["node"] == 2
    return jax.shard_map(
        paired if small else general,
        mesh=mesh,
        in_specs=placed,
        out_specs=P(("rep", "node", "local"), None),
        check_vma=False,
    )
```
